1024 devices in a mesh: grp: 8 (over y, core), dev: 128 (over z, x).
Axes of the slice: x: 4, y: 4, z: 32, core: 2. Of those that a mesh axis runs over, the one named last changes fastest.
Arguments:
- atm_blocks: float32 [8, 128, 8, 64, 128], P('grp', 'dev'), may hold values from -6 to 6
- send_list: int32 [8, 128, 8, 2], P('grp', 'dev'), may hold values from 0 to 7
- weight_src: int32 [8, 128, 4, 8], P('grp', 'dev'), may hold values from 0 to 47
- weights: float32 [8, 128, 4, 8, 128, 128], P('grp', 'dev'), may hold values from -0.1875 to 0.1875
- ocean_nbrs: int32 [8, 128, 4, 4], P('grp', 'dev'), may hold values from 0 to 11
Outputs:
- ocean_fields: float32 [8, 128, 4, 64, 128], P('grp', 'dev')
The draws below stay inside these ranges and needn't reach their ends.
All inputs are finite; a program needn't handle non-finite values.
Results may differ from the reference program's by a relative error of at most 0.0003.
Values sent between devices are 32-bit elements; how exact they have to be, the bound alone decides.
No kernel may reach another device: no remote copies, remote signals or barrier semaphores. Data moves between devices by JAX's collectives and lax.ppermute only.
A program may use at most 32 MiB of HBM per device.

```python
import jax
import jax.numpy as jnp
from jax import lax

BLOCK = 128
FEAT = 64
NA = 8
NO = 4
CAP = 2
K = 8
SWEEPS = 2
N_GRP = 8
N_DEV = 128


def plant(drawn, own_key, smallest, top_value):
    shape = drawn.shape
    spot = [jax.random.randint(jax.random.fold_in(own_key, axis), (), 0, shape[axis]) for axis in range(len(shape))]
    drawn = drawn.at[tuple(spot)].set(smallest)
    longest = shape.index(max(shape))
    spot[longest] = (spot[longest] + 1) % shape[longest]
    return drawn.at[tuple(spot)].set(top_value)


def block_levels(stream_key, dims, shards, least, top_value):
    loudness, own = 1.0, jax.random.fold_in(stream_key, 6)
    for axis_at, parts in shards:
        heights = jnp.exp(jax.random.uniform(jax.random.fold_in(own, axis_at), (parts,), jnp.float32, least / len(shards), top_value / len(shards)))
        loudness = loudness * jnp.repeat(heights, dims[axis_at] // parts).reshape([-1 if axis == axis_at else 1 for axis in range(len(dims))])
    return loudness


def centred(own_key, dims, spread, most, cuts=(), held_as=jnp.bfloat16):
    array = spread * jax.random.normal(own_key, dims, jnp.float32)
    if cuts:
        array = array * block_levels(own_key, dims, cuts, -0.22, 0.18)
    return jnp.clip(array, -most, most).astype(held_as)


def setup_inputs(seed: int = 0) -> dict:
    splits = jax.random.split(jax.random.key(seed), 6)
    return {
        "atm_blocks": centred(splits[0], (N_GRP, N_DEV, NA, FEAT, BLOCK), 1.0, 6.0, ((0, 8), (1, 128)), jnp.float32),
        "send_list": plant(jax.random.randint(splits[1], (N_GRP, N_DEV, N_GRP, CAP), 0, NA), jax.random.fold_in(splits[1], 1), 0, NA - 1).astype(jnp.int32),
        "weight_src": plant(jax.random.randint(splits[2], (N_GRP, N_DEV, NO, K), 0, 3 * N_GRP * CAP), jax.random.fold_in(splits[2], 1), 0, (3 * N_GRP * CAP) - 1).astype(jnp.int32),
        "weights": centred(splits[3], (N_GRP, N_DEV, NO, K, BLOCK, BLOCK), (K * BLOCK) ** -0.5, 0.1875, ((0, 8), (1, 128)), jnp.float32),
        "ocean_nbrs": plant(jax.random.randint(splits[4], (N_GRP, N_DEV, NO, 4), 0, 3 * NO), jax.random.fold_in(splits[4], 1), 0, (3 * NO) - 1).astype(jnp.int32),
    }


def reference(atm_blocks, send_list, weight_src, weights, ocean_nbrs):
    atm_pad = jnp.pad(atm_blocks, ((0, 0), (1, 1), (0, 0), (0, 0), (0, 0)))
    list_pad = jnp.pad(send_list, ((0, 0), (1, 1), (0, 0), (0, 0)))

    def one_device(flat):
        row = flat // N_DEV
        col = flat % N_DEV
        pieces = []
        for offset in range(3):
            blocks = lax.dynamic_index_in_dim(atm_pad, col + offset, 1, keepdims=False)
            chosen = lax.dynamic_index_in_dim(list_pad, col + offset, 1, keepdims=False)
            chosen = lax.dynamic_index_in_dim(chosen, row, 1, keepdims=False)
            picked = jnp.take_along_axis(blocks, chosen[:, :, None, None], axis=1)
            pieces.append(picked)
        pool = jnp.stack(pieces, 1).reshape(3 * N_GRP * CAP, FEAT, BLOCK)
        source = weight_src[row, col]
        gathered = pool[source]
        return jnp.einsum("okfa,okaj->ofj", gathered, weights[row, col], precision=lax.Precision.HIGHEST)

    state = lax.map(one_device, jnp.arange(N_GRP * N_DEV, dtype=jnp.int32))
    state = state.reshape(N_GRP, N_DEV, NO, FEAT, BLOCK)

    def sweep_tile(extended, nbrs, own):
        near = extended[nbrs]
        return own + 0.15 * (jnp.sum(near, axis=1) - 4.0 * own)

    for sweep in range(SWEEPS):
        padded = jnp.pad(state, ((0, 0), (1, 1), (0, 0), (0, 0), (0, 0)))
        extended = jnp.concatenate([padded[:, :-2], padded[:, 1:-1], padded[:, 2:]], axis=2)
        state = jax.vmap(jax.vmap(sweep_tile))(extended, ocean_nbrs, state)
    return state
```

```python
import jax
import jax.numpy as jnp
from jax import lax
from jax.experimental import pallas as pl
from jax.experimental.pallas import tpu as pltpu
from jax.sharding import PartitionSpec as P

QUAD = 4
VMEM = pl.BlockSpec(memory_space=pltpu.VMEM)
SMEM = pl.BlockSpec(memory_space=pltpu.SMEM)
ANY = pl.BlockSpec(memory_space=pl.ANY)
PARAMS = pltpu.CompilerParams(vmem_limit_bytes=24 * 1024 * 1024)


def pick_kernel(lists, atm, out, sems):
    groups, slots = out.shape[0], out.shape[1]
    copies = []
    for g in range(groups):
        for c in range(slots):
            copy = pltpu.make_async_copy(atm.at[lists[g, c]], out.at[g, c], sems.at[g, c])
            copy.start()
            copies.append(copy)
    for copy in copies:
        copy.wait()


def pick(lists, atm):
    groups, slots = lists.shape
    shape = (groups, slots) + atm.shape[1:]
    return pl.pallas_call(
        pick_kernel,
        out_shape=jax.ShapeDtypeStruct(shape, jnp.float32),
        in_specs=[SMEM, ANY],
        out_specs=VMEM,
        scratch_shapes=[pltpu.SemaphoreType.DMA((groups, slots))],
        compiler_params=PARAMS,
        cost_estimate=pl.CostEstimate(flops=0, bytes_accessed=2 * 4 * groups * slots * 64 * 128, transcendentals=0),
        name="pick",
    )(lists, atm)


def halves(x):
    high = x.astype(jnp.bfloat16)
    return high, (x - high.astype(jnp.float32)).astype(jnp.bfloat16)


def remap_kernel(slots, source, low, own, high, weights, out):
    tiles, blocks, cells = weights.shape[0], weights.shape[1], weights.shape[3]
    feat = out.shape[2]
    for b in range(tiles):
        parts = []
        for k in range(blocks):
            p = source[b, k]
            pair = lax.div(p, slots)
            side = lax.rem(pair, 3)
            row = (lax.div(pair, 3) * slots + lax.rem(p, slots)) * feat
            rows = pl.ds(pl.multiple_of(row, feat), feat)
            parts.append(jnp.where(side == 0, low[rows, :], jnp.where(side == 1, own[rows, :], high[rows, :])))
        left = jnp.concatenate(parts, axis=1)
        left_high, left_low = halves(left)
        right_high, right_low = halves(weights[b].reshape(blocks * cells, cells))
        left = jnp.concatenate([left_high, left_low], axis=0)
        right = jnp.concatenate([right_high, right_low], axis=1)
        product = jnp.dot(left, right, preferred_element_type=jnp.float32)
        total = product[:feat, :cells] + (product[:feat, cells:] + product[feat:, :cells])
        for copy in range(out.shape[0]):
            out[copy, b] = total


def remap(source, low, own, high, weights, slots, feat):
    tiles, blocks, depth, cells = weights.shape

    def kernel(*refs):
        remap_kernel(slots, *refs)

    return pl.pallas_call(
        kernel,
        out_shape=jax.ShapeDtypeStruct((QUAD, tiles, feat, cells), jnp.float32),
        in_specs=[SMEM, VMEM, VMEM, VMEM, VMEM],
        out_specs=VMEM,
        compiler_params=PARAMS,
        cost_estimate=pl.CostEstimate(flops=8 * tiles * blocks * feat * depth * cells, bytes_accessed=2**22, transcendentals=0),
        name="remap",
    )(source, low, own, high, weights)


def smooth_kernel(place, nbrs, quad, halo, out, state, first):
    tiles = out.shape[0]
    x, last = place[0], place[1]
    before = jnp.where(x < 2, 2 * tiles, 0)
    behind = jnp.where(x < 2, 0, QUAD * tiles)
    for t in range(QUAD * tiles):
        state[before + t] = quad[t]
    for t in range(2 * tiles):
        state[behind + t] = halo[t]
    centre = before + x * tiles
    degree = nbrs.shape[2]
    for e in range(3):
        for b in range(tiles):
            mine = state[centre + (e - 1) * tiles + b]
            total = None
            for m in range(degree):
                n = nbrs[e, b, m]
                if e == 2:
                    n = jnp.where(last == 1, 3 * tiles - 1, n)
                near = state[centre + (e - 2) * tiles + n]
                total = near if total is None else total + near
            first[e * tiles + b] = mine + 0.15 * (total - 4.0 * mine)
    for b in range(tiles):
        mine = first[tiles + b]
        total = None
        for m in range(degree):
            near = first[nbrs[1, b, m]]
            total = near if total is None else total + near
        out[b] = mine + 0.15 * (total - 4.0 * mine)


def smooth(place, nbrs, quad, halo):
    tiles = nbrs.shape[1]
    feat, cells = quad.shape[1:]
    return pl.pallas_call(
        smooth_kernel,
        out_shape=jax.ShapeDtypeStruct((tiles, feat, cells), jnp.float32),
        in_specs=[SMEM, SMEM, VMEM, VMEM],
        out_specs=VMEM,
        scratch_shapes=[
            pltpu.VMEM(((QUAD + 2) * tiles, feat, cells), jnp.float32),
            pltpu.VMEM((3 * tiles, feat, cells), jnp.float32),
        ],
        compiler_params=PARAMS,
        cost_estimate=pl.CostEstimate(flops=2**20, bytes_accessed=2**20, transcendentals=0),
        name="smooth",
    )(place, nbrs, quad, halo)


def shards(atm_blocks, send_list, weight_src, weights, ocean_nbrs):
    lists = send_list[0, 0]
    nbrs = ocean_nbrs[0, 0]
    groups, slots = lists.shape
    feat, cells = atm_blocks.shape[3:]
    tiles, degree = nbrs.shape
    count = lax.axis_size("dev")
    place = lax.axis_index("dev")
    x = lax.rem(place, QUAD)

    with jax.named_scope("pool"):
        picked = pick(lists, atm_blocks[0, 0])
        arrived = lax.all_to_all(picked, "grp", split_axis=0, concat_axis=0, tiled=True)
        rows = groups * slots * feat
        listed = jnp.pad(nbrs.astype(jnp.float32).reshape(1, tiles * degree), ((0, 7), (0, cells - tiles * degree)))
        own = jnp.concatenate([arrived.reshape(rows, cells), listed], axis=0)
        forward = [(i, i + 1) for i in range(count - 1)]
        backward = [(i + 1, i) for i in range(count - 1)]
        low = lax.ppermute(own, "dev", forward)
        high = lax.ppermute(own, "dev", backward)

    with jax.named_scope("remap"):
        spread = remap(weight_src[0, 0], low, own, high, weights[0, 0], slots, feat)

    with jax.named_scope("halo"):
        rings = [[z * QUAD + i for i in range(QUAD)] for z in range(count // QUAD)]
        quad = lax.all_to_all(spread, "dev", split_axis=0, concat_axis=0, axis_index_groups=rings, tiled=True)
        edge = lax.dynamic_slice_in_dim(quad, jnp.where(x < 2, 2, 0), 2, axis=0)
        hops = []
        for i in range(count):
            target = i + QUAD if i % QUAD < 2 else i - QUAD
            if 0 <= target < count:
                hops.append((i, target))
        halo = lax.ppermute(edge, "dev", hops)

    with jax.named_scope("sweeps"):

        def listed_of(payload):
            return payload[rows, : tiles * degree].astype(jnp.int32).reshape(tiles, degree)

        around = jnp.stack([listed_of(low), nbrs, listed_of(high)])
        position = jnp.stack([x, (place == count - 1).astype(jnp.int32)]).astype(jnp.int32)
        state = smooth(position, around, quad.reshape(QUAD * tiles, feat, cells), halo.reshape(2 * tiles, feat, cells))
    return state[None, None]


def solution(mesh):
    return jax.shard_map(
        shards,
        mesh=mesh,
        in_specs=(
            P("grp", "dev", None, None, None),
            P("grp", "dev", None, None),
            P("grp", "dev", None, None),
            P("grp", "dev", None, None, None, None),
            P("grp", "dev", None, None),
        ),
        out_specs=P("grp", "dev", None, None, None),
        check_vma=False,
    )
```

```python
import functools

import jax
import jax.numpy as jnp
from jax import lax
from jax.experimental import pallas as pl
from jax.experimental.pallas import tpu as pltpu
from jax.sharding import PartitionSpec as P

QUAD = 4
VMEM = pl.BlockSpec(memory_space=pltpu.VMEM)
HBM = pl.BlockSpec(memory_space=pltpu.HBM)
PARAMS = pltpu.CompilerParams(vmem_limit_bytes=24 * 1024 * 1024)


def pick_kernel(lists, atm, out, chosen, blocks, sems):
    first = pltpu.make_async_copy(lists, chosen, sems.at[0])
    second = pltpu.make_async_copy(atm, blocks, sems.at[1])
    first.start()
    second.start()
    first.wait()
    second.wait()
    for g in range(out.shape[0]):
        for c in range(out.shape[1]):
            out[g, c] = blocks[chosen[c, g]]


def pick(lists, atm):
    slots, groups = lists.shape
    return pl.pallas_call(
        pick_kernel,
        out_shape=jax.ShapeDtypeStruct((groups, slots) + atm.shape[1:], jnp.float32),
        in_specs=[HBM, HBM],
        out_specs=VMEM,
        scratch_shapes=[
            pltpu.SMEM(lists.shape, jnp.int32),
            pltpu.VMEM(atm.shape, jnp.float32),
            pltpu.SemaphoreType.DMA((2,)),
        ],
        compiler_params=PARAMS,
        cost_estimate=pl.CostEstimate(flops=0, bytes_accessed=2**19, transcendentals=0),
        name="pick",
    )(pltpu.with_memory_space_constraint(lists, pltpu.HBM), pltpu.with_memory_space_constraint(atm, pltpu.HBM))


def halves(x):
    high = x.astype(jnp.bfloat16)
    return high, (x - high.astype(jnp.float32)).astype(jnp.bfloat16)


def split_kernel(weights, out):
    tiles, blocks, depth, cells = weights.shape
    for b in range(tiles):
        out[b] = jnp.concatenate(halves(weights[b].reshape(blocks * depth, cells)), axis=1)


def split(weights):
    tiles, blocks, depth, cells = weights.shape
    return pl.pallas_call(
        split_kernel,
        out_shape=jax.ShapeDtypeStruct((tiles, blocks * depth, 2 * cells), jnp.bfloat16),
        in_specs=[VMEM],
        out_specs=VMEM,
        compiler_params=PARAMS,
        cost_estimate=pl.CostEstimate(flops=2**20, bytes_accessed=2**22, transcendentals=0),
        name="split",
    )(weights)


def remap_kernel(slots, source, low, own, high, weights, out, pool):
    copies, tiles, feat, cells = out.shape
    entries = pool.shape[0]
    chosen = source[...]
    for side, part in enumerate((low, own, high)):
        for entry in range(entries // 3):
            s, c = divmod(entry, slots)
            pool[(s * 3 + side) * slots + c] = part[entry * feat : (entry + 1) * feat, :]
    for b in range(tiles):
        left = jnp.concatenate([pool[chosen[b, k]] for k in range(source.shape[1])], axis=1)
        left = jnp.concatenate(halves(left), axis=0)
        product = jnp.dot(left, weights[b], preferred_element_type=jnp.float32)
        total = product[:feat, :cells] + (product[:feat, cells:] + product[feat:, :cells])
        for copy in range(copies):
            out[copy, b] = total


def remap(source, low, own, high, weights, groups, slots, feat):
    tiles, depth, width = weights.shape
    cells = width // 2
    return pl.pallas_call(
        functools.partial(remap_kernel, slots),
        out_shape=jax.ShapeDtypeStruct((QUAD, tiles, feat, cells), jnp.float32),
        in_specs=[VMEM] * 5,
        out_specs=VMEM,
        scratch_shapes=[pltpu.VMEM((3 * groups * slots, feat, cells), jnp.float32)],
        compiler_params=PARAMS,
        cost_estimate=pl.CostEstimate(flops=8 * tiles * feat * depth * cells, bytes_accessed=2**22, transcendentals=0),
        name="remap",
    )(source, low, own, high, weights)


def smooth_kernel(index, quad, halo, out, state, first):
    tiles = out.shape[0]
    edge, middle = halo.shape[0], quad.shape[0]
    degree = index.shape[1] // tiles
    spot = index[...]
    for t in range(edge):
        state[t] = halo[t]
        state[edge + middle + t] = halo[t]
    for t in range(middle):
        state[edge + t] = quad[t]
    for e in range(3):
        for b in range(tiles):
            mine = state[spot[4, 0] + (e * tiles + b)]
            total = state[spot[e, b * degree]]
            for m in range(1, degree):
                total = total + state[spot[e, b * degree + m]]
            first[e * tiles + b] = mine + 0.15 * (total - 4.0 * mine)
    for b in range(tiles):
        mine = first[tiles + b]
        total = first[spot[3, b * degree]]
        for m in range(1, degree):
            total = total + first[spot[3, b * degree + m]]
        out[b] = mine + 0.15 * (total - 4.0 * mine)


def smooth(index, quad, halo):
    middle, feat, cells = quad.shape
    tiles = middle // QUAD
    edge = halo.shape[0]
    return pl.pallas_call(
        smooth_kernel,
        out_shape=jax.ShapeDtypeStruct((tiles, feat, cells), jnp.float32),
        in_specs=[VMEM, VMEM, VMEM],
        out_specs=VMEM,
        scratch_shapes=[
            pltpu.VMEM((edge + middle + edge, feat, cells), jnp.float32),
            pltpu.VMEM((3 * tiles, feat, cells), jnp.float32),
        ],
        compiler_params=PARAMS,
        cost_estimate=pl.CostEstimate(flops=2**20, bytes_accessed=2**20, transcendentals=0),
        name="smooth",
    )(index, quad, halo)


def shards(atm_blocks, send_list, weight_src, weights, ocean_nbrs):
    lists = send_list[0, 0]
    nbrs = ocean_nbrs[0, 0]
    groups, slots = lists.shape
    feat, cells = atm_blocks.shape[3:]
    tiles, degree = nbrs.shape
    count = lax.axis_size("dev")
    place = lax.axis_index("dev")
    x = lax.rem(place, QUAD)

    with jax.named_scope("pool"):
        picked = pick(lists.T, atm_blocks[0, 0])
        arrived = lax.all_to_all(picked, "grp", split_axis=0, concat_axis=0, tiled=True)
        rows = groups * slots * feat
        listed = jnp.pad(nbrs.astype(jnp.float32).reshape(1, tiles * degree), ((0, 7), (0, cells - tiles * degree)))
        own = jnp.concatenate([arrived.reshape(rows, cells), listed], axis=0)
        forward = [(i, i + 1) for i in range(count - 1)]
        backward = [(i + 1, i) for i in range(count - 1)]
        low = lax.ppermute(own, "dev", forward)
        high = lax.ppermute(own, "dev", backward)

    with jax.named_scope("remap"):
        spread = remap(weight_src[0, 0], low, own, high, split(weights[0, 0]), groups, slots, feat)

    with jax.named_scope("halo"):
        rings = [[z * QUAD + i for i in range(QUAD)] for z in range(count // QUAD)]
        quad = lax.all_to_all(spread, "dev", split_axis=0, concat_axis=0, axis_index_groups=rings, tiled=True)
        edge = lax.dynamic_slice_in_dim(quad, jnp.where(x < 2, 2, 0), 2, axis=0)
        hops = []
        for i in range(count):
            target = i + QUAD if i % QUAD < 2 else i - QUAD
            if 0 <= target < count:
                hops.append((i, target))
        halo = lax.ppermute(edge, "dev", hops)

    with jax.named_scope("sweeps"):

        def listed_of(payload):
            return payload[rows : rows + 1, : tiles * degree].astype(jnp.int32)

        centre = 2 * tiles + x * tiles
        after = jnp.where(place == count - 1, 3 * tiles - 1, listed_of(high))
        mine = nbrs.reshape(1, tiles * degree)
        index = jnp.concatenate(
            [
                listed_of(low) + (centre - 2 * tiles),
                mine + (centre - tiles),
                after + centre,
                mine,
                jnp.full((1, tiles * degree), centre - tiles, jnp.int32),
            ],
            axis=0,
        )
        state = smooth(index, quad.reshape(QUAD * tiles, feat, cells), halo.reshape(2 * tiles, feat, cells))
    return state[None, None]


def solution(mesh):
    return jax.shard_map(
        shards,
        mesh=mesh,
        in_specs=(
            P("grp", "dev", None, None, None),
            P("grp", "dev", None, None),
            P("grp", "dev", None, None),
            P("grp", "dev", None, None, None, None),
            P("grp", "dev", None, None),
        ),
        out_specs=P("grp", "dev", None, None, None),
        check_vma=False,
    )
```

```python
import functools

import jax
import jax.numpy as jnp
from jax import lax
from jax.experimental import pallas as pl
from jax.experimental.pallas import tpu as pltpu
from jax.sharding import PartitionSpec as P

QUAD = 4
VMEM = pl.BlockSpec(memory_space=pltpu.VMEM)
HBM = pl.BlockSpec(memory_space=pltpu.HBM)
PARAMS = pltpu.CompilerParams(vmem_limit_bytes=24 * 1024 * 1024)


def pick_kernel(lists, atm, *rest):
    outs, (chosen, blocks, sems) = rest[:-3], rest[-3:]
    first = pltpu.make_async_copy(lists, chosen, sems.at[0])
    second = pltpu.make_async_copy(atm, blocks, sems.at[1])
    first.start()
    second.start()
    first.wait()
    second.wait()
    for c, out in enumerate(outs):
        for g in range(out.shape[0]):
            out[g] = blocks[chosen[c, g]]


def pick(lists, atm):
    slots, groups = lists.shape
    return pl.pallas_call(
        pick_kernel,
        out_shape=[jax.ShapeDtypeStruct((groups,) + atm.shape[1:], jnp.float32)] * slots,
        in_specs=[HBM, HBM],
        out_specs=[VMEM] * slots,
        scratch_shapes=[
            pltpu.SMEM(lists.shape, jnp.int32),
            pltpu.VMEM(atm.shape, jnp.float32),
            pltpu.SemaphoreType.DMA((2,)),
        ],
        compiler_params=PARAMS,
        cost_estimate=pl.CostEstimate(flops=0, bytes_accessed=2**19, transcendentals=0),
        name="pick",
    )(pltpu.with_memory_space_constraint(lists, pltpu.HBM), pltpu.with_memory_space_constraint(atm, pltpu.HBM))


def halves(x):
    high = x.astype(jnp.bfloat16)
    return high, (x - high.astype(jnp.float32)).astype(jnp.bfloat16)


def split_kernel(weights, out):
    tiles, blocks, depth, cells = weights.shape
    for b in range(tiles):
        out[b] = jnp.concatenate(halves(weights[b].reshape(blocks * depth, cells)), axis=1)


def split(weights):
    tiles, blocks, depth, cells = weights.shape
    return pl.pallas_call(
        split_kernel,
        out_shape=jax.ShapeDtypeStruct((tiles, blocks * depth, 2 * cells), jnp.bfloat16),
        in_specs=[VMEM],
        out_specs=VMEM,
        compiler_params=PARAMS,
        cost_estimate=pl.CostEstimate(flops=2**20, bytes_accessed=2**22, transcendentals=0),
        name="split",
    )(weights)


def remap_kernel(slots, source, *rest):
    parts, (weights, out, pool) = rest[:-3], rest[-3:]
    copies, tiles, feat, cells = out.shape
    chosen = source[...]
    for at, part in enumerate(parts):
        for s in range(pool.shape[0] // (3 * slots)):
            pool[s * 3 * slots + at] = part[s * feat : (s + 1) * feat, :]
    for b in range(tiles):
        left = jnp.concatenate([pool[chosen[b, k]] for k in range(source.shape[1])], axis=1)
        left = jnp.concatenate(halves(left), axis=0)
        product = jnp.dot(left, weights[b], preferred_element_type=jnp.float32)
        total = product[:feat, :cells] + (product[:feat, cells:] + product[feat:, :cells])
        for copy in range(copies):
            out[copy, b] = total


def remap(source, parts, weights, groups, feat):
    tiles, depth, width = weights.shape
    cells = width // 2
    return pl.pallas_call(
        functools.partial(remap_kernel, len(parts) // 3),
        out_shape=jax.ShapeDtypeStruct((QUAD, tiles, feat, cells), jnp.float32),
        in_specs=[VMEM] * (len(parts) + 2),
        out_specs=VMEM,
        scratch_shapes=[pltpu.VMEM((groups * len(parts), feat, cells), jnp.float32)],
        compiler_params=PARAMS,
        cost_estimate=pl.CostEstimate(flops=8 * tiles * feat * depth * cells, bytes_accessed=2**22, transcendentals=0),
        name="remap",
    )(source, *parts, weights)


def smooth_kernel(index, quad, halo, out, state, first):
    tiles = out.shape[0]
    edge, middle = halo.shape[0], quad.shape[0]
    degree = index.shape[1] // tiles
    spot = index[...]
    for t in range(edge):
        state[t] = halo[t]
        state[edge + middle + t] = halo[t]
    for t in range(middle):
        state[edge + t] = quad[t]
    for e in range(3):
        for b in range(tiles):
            mine = state[spot[4, 0] + (e * tiles + b)]
            total = state[spot[e, b * degree]]
            for m in range(1, degree):
                total = total + state[spot[e, b * degree + m]]
            first[e * tiles + b] = mine + 0.15 * (total - 4.0 * mine)
    for b in range(tiles):
        mine = first[tiles + b]
        total = first[spot[3, b * degree]]
        for m in range(1, degree):
            total = total + first[spot[3, b * degree + m]]
        out[b] = mine + 0.15 * (total - 4.0 * mine)


def smooth(index, quad, halo):
    middle, feat, cells = quad.shape
    tiles = middle // QUAD
    edge = halo.shape[0]
    return pl.pallas_call(
        smooth_kernel,
        out_shape=jax.ShapeDtypeStruct((tiles, feat, cells), jnp.float32),
        in_specs=[VMEM, VMEM, VMEM],
        out_specs=VMEM,
        scratch_shapes=[
            pltpu.VMEM((edge + middle + edge, feat, cells), jnp.float32),
            pltpu.VMEM((3 * tiles, feat, cells), jnp.float32),
        ],
        compiler_params=PARAMS,
        cost_estimate=pl.CostEstimate(flops=2**20, bytes_accessed=2**20, transcendentals=0),
        name="smooth",
    )(index, quad, halo)


def shards(atm_blocks, send_list, weight_src, weights, ocean_nbrs):
    lists = send_list[0, 0]
    nbrs = ocean_nbrs[0, 0]
    groups, slots = lists.shape
    feat, cells = atm_blocks.shape[3:]
    tiles, degree = nbrs.shape
    count = lax.axis_size("dev")
    place = lax.axis_index("dev")
    x = lax.rem(place, QUAD)

    with jax.named_scope("pool"):
        picked = pick(lists.T, atm_blocks[0, 0])
        listed = jnp.pad(nbrs.astype(jnp.float32).reshape(1, tiles * degree), ((0, 7), (0, cells - tiles * degree)))
        forward = [(i, i + 1) for i in range(count - 1)]
        backward = [(i + 1, i) for i in range(count - 1)]
        low, own, high = [], [], []
        for c in range(slots):
            arrived = lax.all_to_all(picked[c], "grp", split_axis=0, concat_axis=0, tiled=True)
            arrived = arrived.reshape(groups * feat, cells)
            own.append(jnp.concatenate([arrived, listed], axis=0) if c == 0 else arrived)
        for c in range(slots):
            low.append(lax.ppermute(own[c], "dev", forward))
            high.append(lax.ppermute(own[c], "dev", backward))

    with jax.named_scope("remap"):
        spread = remap(weight_src[0, 0], low + own + high, split(weights[0, 0]), groups, feat)

    with jax.named_scope("halo"):
        rings = [[z * QUAD + i for i in range(QUAD)] for z in range(count // QUAD)]
        quad = lax.all_to_all(spread, "dev", split_axis=0, concat_axis=0, axis_index_groups=rings, tiled=True)
        edge = lax.dynamic_slice_in_dim(quad, jnp.where(x < 2, 2, 0), 2, axis=0)
        hops = []
        for i in range(count):
            target = i + QUAD if i % QUAD < 2 else i - QUAD
            if 0 <= target < count:
                hops.append((i, target))
        halo = lax.ppermute(edge, "dev", hops)

    with jax.named_scope("sweeps"):

        def listed_of(payload):
            return payload[groups * feat : groups * feat + 1, : tiles * degree].astype(jnp.int32)

        centre = 2 * tiles + x * tiles
        after = jnp.where(place == count - 1, 3 * tiles - 1, listed_of(high[0]))
        mine = nbrs.reshape(1, tiles * degree)
        index = jnp.concatenate(
            [
                listed_of(low[0]) + (centre - 2 * tiles),
                mine + (centre - tiles),
                after + centre,
                mine,
                jnp.full((1, tiles * degree), centre - tiles, jnp.int32),
            ],
            axis=0,
        )
        state = smooth(index, quad.reshape(QUAD * tiles, feat, cells), halo.reshape(2 * tiles, feat, cells))
    return state[None, None]


def solution(mesh):
    return jax.shard_map(
        shards,
        mesh=mesh,
        in_specs=(
            P("grp", "dev", None, None, None),
            P("grp", "dev", None, None),
            P("grp", "dev", None, None),
            P("grp", "dev", None, None, None, None),
            P("grp", "dev", None, None),
        ),
        out_specs=P("grp", "dev", None, None, None),
        check_vma=False,
    )
```

```python
import functools

import jax
import jax.numpy as jnp
from jax import lax
from jax.experimental import pallas as pl
from jax.experimental.pallas import tpu as pltpu
from jax.sharding import PartitionSpec as P

QUAD = 4
VMEM = pl.BlockSpec(memory_space=pltpu.VMEM)
HBM = pl.BlockSpec(memory_space=pltpu.HBM)
PARAMS = pltpu.CompilerParams(vmem_limit_bytes=24 * 1024 * 1024)


def pick_kernel(lists, atm, out, chosen, blocks, sems):
    first = pltpu.make_async_copy(lists, chosen, sems.at[0])
    second = pltpu.make_async_copy(atm, blocks, sems.at[1])
    first.start()
    second.start()
    first.wait()
    second.wait()
    for g in range(out.shape[0]):
        for c in range(out.shape[1]):
            out[g, c] = blocks[chosen[c, g]]


def pick(lists, atm):
    slots, groups = lists.shape
    return pl.pallas_call(
        pick_kernel,
        out_shape=jax.ShapeDtypeStruct((groups, slots) + atm.shape[1:], jnp.float32),
        in_specs=[HBM, HBM],
        out_specs=VMEM,
        scratch_shapes=[
            pltpu.SMEM(lists.shape, jnp.int32),
            pltpu.VMEM(atm.shape, jnp.float32),
            pltpu.SemaphoreType.DMA((2,)),
        ],
        compiler_params=PARAMS,
        cost_estimate=pl.CostEstimate(flops=0, bytes_accessed=2**19, transcendentals=0),
        name="pick",
    )(pltpu.with_memory_space_constraint(lists, pltpu.HBM), pltpu.with_memory_space_constraint(atm, pltpu.HBM))


def halves(x):
    high = x.astype(jnp.bfloat16)
    return high, (x - high.astype(jnp.float32)).astype(jnp.bfloat16)


def split_kernel(weights, out):
    tiles, blocks, depth, cells = weights.shape
    for b in range(tiles):
        out[b] = jnp.concatenate(halves(weights[b].reshape(blocks * depth, cells)), axis=1)


def split(weights):
    tiles, blocks, depth, cells = weights.shape
    return pl.pallas_call(
        split_kernel,
        out_shape=jax.ShapeDtypeStruct((tiles, blocks * depth, 2 * cells), jnp.bfloat16),
        in_specs=[VMEM],
        out_specs=VMEM,
        compiler_params=PARAMS,
        cost_estimate=pl.CostEstimate(flops=2**20, bytes_accessed=2**22, transcendentals=0),
        name="split",
    )(weights)


def remap_kernel(slots, source, low, own, high, weights, out, spread, pool):
    copies, tiles, feat, cells = spread.shape
    entries = pool.shape[0]
    chosen = source[...]
    for side, part in enumerate((low, own, high)):
        for entry in range(entries // 3):
            s, c = divmod(entry, slots)
            pool[(s * 3 + side) * slots + c] = part[entry * feat : (entry + 1) * feat, :]
    for b in range(tiles):
        left = jnp.concatenate([pool[chosen[b, k]] for k in range(source.shape[1])], axis=1)
        left = jnp.concatenate(halves(left), axis=0)
        product = jnp.dot(left, weights[b], preferred_element_type=jnp.float32)
        total = product[:feat, :cells] + (product[:feat, cells:] + product[feat:, :cells])
        out[b] = total
        for copy in range(copies):
            spread[copy, b] = total


def remap(source, low, own, high, weights, groups, slots, feat):
    tiles, depth, width = weights.shape
    cells = width // 2
    return pl.pallas_call(
        functools.partial(remap_kernel, slots),
        out_shape=[
            jax.ShapeDtypeStruct((tiles, feat, cells), jnp.float32),
            jax.ShapeDtypeStruct((QUAD, tiles, feat, cells), jnp.float32),
        ],
        in_specs=[VMEM] * 5,
        out_specs=[VMEM, VMEM],
        scratch_shapes=[pltpu.VMEM((3 * groups * slots, feat, cells), jnp.float32)],
        compiler_params=PARAMS,
        cost_estimate=pl.CostEstimate(flops=8 * tiles * feat * depth * cells, bytes_accessed=2**22, transcendentals=0),
        name="remap",
    )(source, low, own, high, weights)


def smooth_kernel(index, quad, near, far, out, state, first):
    tiles = out.shape[0]
    middle = quad.shape[0]
    degree = index.shape[1] // tiles
    spot = index[...]
    inner = spot[4, 1] == 1
    for t in range(tiles):
        state[t] = far[t]
        state[3 * tiles + middle + t] = far[t]
        beside = jnp.where(inner, far[t], near[t])
        state[tiles + t] = beside
        state[2 * tiles + middle + t] = beside
    for t in range(middle):
        state[2 * tiles + t] = quad[t]
    for e in range(3):
        for b in range(tiles):
            mine = state[spot[4, 0] + (e * tiles + b)]
            total = state[spot[e, b * degree]]
            for m in range(1, degree):
                total = total + state[spot[e, b * degree + m]]
            first[e * tiles + b] = mine + 0.15 * (total - 4.0 * mine)
    for b in range(tiles):
        mine = first[tiles + b]
        total = first[spot[3, b * degree]]
        for m in range(1, degree):
            total = total + first[spot[3, b * degree + m]]
        out[b] = mine + 0.15 * (total - 4.0 * mine)


def smooth(index, quad, near, far):
    middle, feat, cells = quad.shape
    tiles = middle // QUAD
    return pl.pallas_call(
        smooth_kernel,
        out_shape=jax.ShapeDtypeStruct((tiles, feat, cells), jnp.float32),
        in_specs=[VMEM] * 4,
        out_specs=VMEM,
        scratch_shapes=[
            pltpu.VMEM((middle + 4 * tiles, feat, cells), jnp.float32),
            pltpu.VMEM((3 * tiles, feat, cells), jnp.float32),
        ],
        compiler_params=PARAMS,
        cost_estimate=pl.CostEstimate(flops=2**20, bytes_accessed=2**20, transcendentals=0),
        name="smooth",
    )(index, quad, near, far)


def shards(atm_blocks, send_list, weight_src, weights, ocean_nbrs):
    lists = send_list[0, 0]
    nbrs = ocean_nbrs[0, 0]
    groups, slots = lists.shape
    feat, cells = atm_blocks.shape[3:]
    tiles, degree = nbrs.shape
    count = lax.axis_size("dev")
    place = lax.axis_index("dev")
    x = lax.rem(place, QUAD)

    with jax.named_scope("pool"):
        picked = pick(lists.T, atm_blocks[0, 0])
        arrived = lax.all_to_all(picked, "grp", split_axis=0, concat_axis=0, tiled=True)
        rows = groups * slots * feat
        listed = jnp.pad(nbrs.astype(jnp.float32).reshape(1, tiles * degree), ((0, 7), (0, cells - tiles * degree)))
        own = jnp.concatenate([arrived.reshape(rows, cells), listed], axis=0)
        forward = [(i, i + 1) for i in range(count - 1)]
        backward = [(i + 1, i) for i in range(count - 1)]
        low = lax.ppermute(own, "dev", forward)
        high = lax.ppermute(own, "dev", backward)

    with jax.named_scope("remap"):
        state, spread = remap(weight_src[0, 0], low, own, high, split(weights[0, 0]), groups, slots, feat)

    with jax.named_scope("halo"):
        ends, twos = [], []
        for start in range(QUAD, count, QUAD):
            ends += [(start - 1, start), (start, start - 1)]
            for i in (start - 2, start - 1):
                twos += [(i, i + 2), (i + 2, i)]
        near = lax.ppermute(state, "dev", ends)
        far = lax.ppermute(state, "dev", twos)
        rings = [[z * QUAD + i for i in range(QUAD)] for z in range(count // QUAD)]
        quad = lax.all_to_all(spread, "dev", split_axis=0, concat_axis=0, axis_index_groups=rings, tiled=True)

    with jax.named_scope("sweeps"):

        def listed_of(payload):
            return payload[rows : rows + 1, : tiles * degree].astype(jnp.int32)

        centre = 2 * tiles + x * tiles
        after = jnp.where(place == count - 1, 3 * tiles - 1, listed_of(high))
        mine = nbrs.reshape(1, tiles * degree)
        index = jnp.concatenate(
            [
                listed_of(low) + (centre - 2 * tiles),
                mine + (centre - tiles),
                after + centre,
                mine,
                jnp.where(jnp.arange(tiles * degree) == 1, (x % 3 != 0).astype(jnp.int32), centre - tiles)[None],
            ],
            axis=0,
        )
        state = smooth(index, quad.reshape(QUAD * tiles, feat, cells), near, far)
    return state[None, None]


def solution(mesh):
    return jax.shard_map(
        shards,
        mesh=mesh,
        in_specs=(
            P("grp", "dev", None, None, None),
            P("grp", "dev", None, None),
            P("grp", "dev", None, None),
            P("grp", "dev", None, None, None, None),
            P("grp", "dev", None, None),
        ),
        out_specs=P("grp", "dev", None, None, None),
        check_vma=False,
    )
```

```python
import functools

import jax
import jax.numpy as jnp
from jax import lax
from jax.experimental import pallas as pl
from jax.experimental.pallas import tpu as pltpu
from jax.sharding import PartitionSpec as P

QUAD = 4
VMEM = pl.BlockSpec(memory_space=pltpu.VMEM)
HBM = pl.BlockSpec(memory_space=pltpu.HBM)
PARAMS = pltpu.CompilerParams(vmem_limit_bytes=24 * 1024 * 1024)


def pick_kernel(lists, atm, out, chosen, blocks, sems):
    first = pltpu.make_async_copy(lists, chosen, sems.at[0])
    second = pltpu.make_async_copy(atm, blocks, sems.at[1])
    first.start()
    second.start()
    first.wait()
    second.wait()
    for g in range(out.shape[0]):
        for c in range(out.shape[1]):
            out[g, c] = blocks[chosen[c, g]]


def pick(lists, atm):
    slots, groups = lists.shape
    return pl.pallas_call(
        pick_kernel,
        out_shape=jax.ShapeDtypeStruct((groups, slots) + atm.shape[1:], jnp.float32),
        in_specs=[HBM, HBM],
        out_specs=VMEM,
        scratch_shapes=[
            pltpu.SMEM(lists.shape, jnp.int32),
            pltpu.VMEM(atm.shape, jnp.float32),
            pltpu.SemaphoreType.DMA((2,)),
        ],
        compiler_params=PARAMS,
        cost_estimate=pl.CostEstimate(flops=0, bytes_accessed=2**19, transcendentals=0),
        name="pick",
    )(pltpu.with_memory_space_constraint(lists, pltpu.HBM), pltpu.with_memory_space_constraint(atm, pltpu.HBM))


def halves(x):
    high = x.astype(jnp.bfloat16)
    return high, (x - high.astype(jnp.float32)).astype(jnp.bfloat16)


def split_kernel(weights, out):
    tiles, blocks, depth, cells = weights.shape
    for b in range(tiles):
        out[b] = jnp.concatenate(halves(weights[b].reshape(blocks * depth, cells)), axis=1)


def split(weights):
    tiles, blocks, depth, cells = weights.shape
    return pl.pallas_call(
        split_kernel,
        out_shape=jax.ShapeDtypeStruct((tiles, blocks * depth, 2 * cells), jnp.bfloat16),
        in_specs=[VMEM],
        out_specs=VMEM,
        compiler_params=PARAMS,
        cost_estimate=pl.CostEstimate(flops=2**20, bytes_accessed=2**22, transcendentals=0),
        name="split",
    )(weights)


def remap_kernel(slots, source, first, own, second, weights, out, pool):
    tiles, feat, cells = out.shape
    entries = pool.shape[0]
    chosen = source[...]
    swap = 2 * (1 - lax.rem(lax.axis_index("dev"), 2))
    for side, part in ((swap, first), (1, own), (2 - swap, second)):
        for entry in range(entries // 3):
            s, c = divmod(entry, slots)
            pool[(s * 3 + side) * slots + c] = part[entry * feat : (entry + 1) * feat, :]
    for b in range(tiles):
        left = jnp.concatenate([pool[chosen[b, k]] for k in range(source.shape[1])], axis=1)
        left = jnp.concatenate(halves(left), axis=0)
        product = jnp.dot(left, weights[b], preferred_element_type=jnp.float32)
        total = product[:feat, :cells] + (product[:feat, cells:] + product[feat:, :cells])
        out[b] = total


def remap(source, first, own, second, weights, groups, slots, feat):
    tiles, depth, width = weights.shape
    cells = width // 2
    return pl.pallas_call(
        functools.partial(remap_kernel, slots),
        out_shape=jax.ShapeDtypeStruct((tiles, feat, cells), jnp.float32),
        in_specs=[VMEM] * 5,
        out_specs=VMEM,
        scratch_shapes=[pltpu.VMEM((3 * groups * slots, feat, cells), jnp.float32)],
        compiler_params=PARAMS,
        cost_estimate=pl.CostEstimate(flops=8 * tiles * feat * depth * cells, bytes_accessed=2**22, transcendentals=0),
        name="remap",
    )(source, first, own, second, weights)


def smooth_kernel(index, own, inner, ring, outer, across, out, state, first):
    tiles = out.shape[0]
    degree = index.shape[1] // tiles
    spot = index[...]
    place = lax.axis_index("dev")
    odd = lax.rem(place, 2) == 1
    upper = lax.rem(place, QUAD) >= 2
    for t in range(tiles):
        state[t] = jnp.where(upper, ring[t], across[t])
        state[tiles + t] = jnp.where(odd, inner[t], outer[t])
        state[2 * tiles + t] = own[t]
        state[3 * tiles + t] = jnp.where(odd, outer[t], inner[t])
        state[4 * tiles + t] = jnp.where(upper, across[t], ring[t])
    for e in range(3):
        for b in range(tiles):
            mine = state[(e + 1) * tiles + b]
            total = state[spot[e, b * degree]]
            for m in range(1, degree):
                total = total + state[spot[e, b * degree + m]]
            first[e * tiles + b] = mine + 0.15 * (total - 4.0 * mine)
    for b in range(tiles):
        mine = first[tiles + b]
        total = first[spot[3, b * degree]]
        for m in range(1, degree):
            total = total + first[spot[3, b * degree + m]]
        out[b] = mine + 0.15 * (total - 4.0 * mine)


def smooth(index, *parts):
    tiles, feat, cells = parts[0].shape
    return pl.pallas_call(
        smooth_kernel,
        out_shape=jax.ShapeDtypeStruct((tiles, feat, cells), jnp.float32),
        in_specs=[VMEM] * (1 + len(parts)),
        out_specs=VMEM,
        scratch_shapes=[
            pltpu.VMEM((5 * tiles, feat, cells), jnp.float32),
            pltpu.VMEM((3 * tiles, feat, cells), jnp.float32),
        ],
        compiler_params=PARAMS,
        cost_estimate=pl.CostEstimate(flops=2**20, bytes_accessed=2**20, transcendentals=0),
        name="smooth",
    )(index, *parts)


def shards(atm_blocks, send_list, weight_src, weights, ocean_nbrs):
    lists = send_list[0, 0]
    nbrs = ocean_nbrs[0, 0]
    groups, slots = lists.shape
    feat, cells = atm_blocks.shape[3:]
    tiles, degree = nbrs.shape
    count = lax.axis_size("dev")
    place = lax.axis_index("dev")
    x = lax.rem(place, QUAD)

    with jax.named_scope("pool"):
        picked = pick(lists.T, atm_blocks[0, 0])
        arrived = lax.all_to_all(picked, "grp", split_axis=0, concat_axis=0, tiled=True)
        rows = groups * slots * feat
        listed = jnp.pad(nbrs.astype(jnp.float32).reshape(1, tiles * degree), ((0, 7), (0, cells - tiles * degree)))
        own = jnp.concatenate([arrived.reshape(rows, cells), listed], axis=0)
        first = lax.ppermute(own, "dev", [(i, i ^ 1) for i in range(count)])
        second = lax.ppermute(own, "dev", [(i, ((i + 1) ^ 1) - 1) for i in range(1, count - 1)])
        odd = lax.rem(place, 2) == 1

    with jax.named_scope("remap"):
        first_list = first[rows : rows + 1, : tiles * degree]
        second_list = second[rows : rows + 1, : tiles * degree]
        low_list = jnp.where(odd, first_list, second_list)
        high_list = jnp.where(odd, second_list, first_list)
        state = remap(weight_src[0, 0], first, own, second, split(pltpu.with_memory_space_constraint(weights[0, 0], pltpu.HBM)), groups, slots, feat)

    with jax.named_scope("halo"):
        inner = lax.ppermute(state, "dev", [(i, i ^ 1) for i in range(count)])
        ring = lax.ppermute(state, "dev", [(i, i ^ 2) for i in range(count)])
        outer = lax.ppermute(state, "dev", [(i, ((i + 1) ^ 1) - 1) for i in range(1, count - 1)])
        across = lax.ppermute(state, "dev", [(i, ((i + 2) ^ 2) - 2) for i in range(2, count - 2)])

    with jax.named_scope("sweeps"):

        def listed_of(payload):
            return payload[rows : rows + 1, : tiles * degree].astype(jnp.int32)

        after = jnp.where(place == count - 1, 3 * tiles - 1, high_list.astype(jnp.int32))
        mine = nbrs.reshape(1, tiles * degree)
        index = jnp.concatenate([low_list.astype(jnp.int32), mine + tiles, after + 2 * tiles, mine], axis=0)
        state = smooth(index, state, inner, ring, outer, across)
    return state[None, None]


def solution(mesh):
    return jax.shard_map(
        shards,
        mesh=mesh,
        in_specs=(
            P("grp", "dev", None, None, None),
            P("grp", "dev", None, None),
            P("grp", "dev", None, None),
            P("grp", "dev", None, None, None, None),
            P("grp", "dev", None, None),
        ),
        out_specs=P("grp", "dev", None, None, None),
        check_vma=False,
    )
```

```python
import functools

import jax
import jax.numpy as jnp
from jax import lax
from jax.experimental import pallas as pl
from jax.experimental.pallas import tpu as pltpu
from jax.sharding import PartitionSpec as P

QUAD = 4
VMEM = pl.BlockSpec(memory_space=pltpu.VMEM)
HBM = pl.BlockSpec(memory_space=pltpu.HBM)
PARAMS = pltpu.CompilerParams(vmem_limit_bytes=24 * 1024 * 1024)


def pick_kernel(lists, nbrs, atm, out, listed, chosen, beside, blocks, sems):
    first = pltpu.make_async_copy(lists, chosen, sems.at[0])
    second = pltpu.make_async_copy(nbrs, beside, sems.at[1])
    third = pltpu.make_async_copy(atm, blocks, sems.at[2])
    first.start()
    second.start()
    third.start()
    first.wait()
    second.wait()
    lane = lax.broadcasted_iota(jnp.int32, listed.shape, 1)
    row = jnp.zeros(listed.shape, jnp.int32)
    tiles, degree = beside.shape
    for b in range(tiles):
        for m in range(degree):
            row = jnp.where(lane == b * degree + m, beside[b, m], row)
    listed[...] = row.astype(jnp.float32)
    third.wait()
    for g in range(out.shape[0]):
        for c in range(out.shape[1]):
            out[g, c] = blocks[chosen[c, g]]


def pick(lists, nbrs, atm):
    slots, groups = lists.shape
    inputs = (pltpu.with_memory_space_constraint(a, pltpu.HBM) for a in (lists, nbrs, atm))
    return pl.pallas_call(
        pick_kernel,
        out_shape=[
            jax.ShapeDtypeStruct((groups, slots) + atm.shape[1:], jnp.float32),
            jax.ShapeDtypeStruct((8, atm.shape[2]), jnp.float32),
        ],
        in_specs=[HBM, HBM, HBM],
        out_specs=[VMEM, VMEM],
        scratch_shapes=[
            pltpu.SMEM(lists.shape, jnp.int32),
            pltpu.SMEM(nbrs.shape, jnp.int32),
            pltpu.VMEM(atm.shape, jnp.float32),
            pltpu.SemaphoreType.DMA((3,)),
        ],
        compiler_params=PARAMS,
        cost_estimate=pl.CostEstimate(flops=0, bytes_accessed=2**19, transcendentals=0),
        name="pick",
    )(*inputs)


def halves(x):
    high = x.astype(jnp.bfloat16)
    return high, (x - high.astype(jnp.float32)).astype(jnp.bfloat16)


def split_kernel(weights, out):
    tiles, blocks, depth, cells = weights.shape
    for b in range(tiles):
        out[b] = jnp.concatenate(halves(weights[b].reshape(blocks * depth, cells)), axis=1)


def split(weights):
    tiles, blocks, depth, cells = weights.shape
    return pl.pallas_call(
        split_kernel,
        out_shape=jax.ShapeDtypeStruct((tiles, blocks * depth, 2 * cells), jnp.bfloat16),
        in_specs=[VMEM],
        out_specs=VMEM,
        compiler_params=PARAMS,
        cost_estimate=pl.CostEstimate(flops=2**20, bytes_accessed=2**22, transcendentals=0),
        name="split",
    )(weights)


def remap_kernel(slots, source, first, own, second, weights, out, pool):
    tiles, feat, cells = out.shape
    entries = pool.shape[0]
    chosen = source[...]
    swap = 2 * (1 - lax.rem(lax.axis_index("dev"), 2))
    for side, part in ((swap, first), (1, own), (2 - swap, second)):
        for entry in range(entries // 3):
            s, c = divmod(entry, slots)
            pool[(s * 3 + side) * slots + c] = part[entry * feat : (entry + 1) * feat, :]
    for b in range(tiles):
        left = jnp.concatenate([pool[chosen[b, k]] for k in range(source.shape[1])], axis=1)
        left = jnp.concatenate(halves(left), axis=0)
        product = jnp.dot(left, weights[b], preferred_element_type=jnp.float32)
        total = product[:feat, :cells] + (product[:feat, cells:] + product[feat:, :cells])
        out[b] = total


def remap(source, first, own, second, weights, groups, slots, feat):
    tiles, depth, width = weights.shape
    cells = width // 2
    return pl.pallas_call(
        functools.partial(remap_kernel, slots),
        out_shape=jax.ShapeDtypeStruct((tiles, feat, cells), jnp.float32),
        in_specs=[VMEM] * 5,
        out_specs=VMEM,
        scratch_shapes=[pltpu.VMEM((3 * groups * slots, feat, cells), jnp.float32)],
        compiler_params=PARAMS,
        cost_estimate=pl.CostEstimate(flops=8 * tiles * feat * depth * cells, bytes_accessed=2**22, transcendentals=0),
        name="remap",
    )(source, first, own, second, weights)


def smooth_kernel(index, own, inner, ring, across, outer, out, state, first):
    tiles = out.shape[0]
    degree = index.shape[1] // tiles
    pair, other, mine = (index[row : row + 1, :] for row in range(3))
    place = lax.axis_index("dev")
    odd = lax.rem(place, 2) == 1
    upper = lax.rem(place, QUAD) >= 2
    after = jnp.where(odd, other, pair)
    after = jnp.where(place == lax.axis_size("dev") - 1, 3 * tiles - 1, after)
    lists = (jnp.where(odd, pair, other), mine, after)
    for t in range(tiles):
        state[t] = jnp.where(upper, ring[t], across[t])
        state[tiles + t] = jnp.where(odd, inner[t], outer[t])
        state[2 * tiles + t] = own[t]
        state[3 * tiles + t] = jnp.where(odd, outer[t], inner[t])
        state[4 * tiles + t] = jnp.where(upper, across[t], ring[t])
    for e in range(3):
        for b in range(tiles):
            here = state[(e + 1) * tiles + b]
            total = state[e * tiles + lists[e][0, b * degree]]
            for m in range(1, degree):
                total = total + state[e * tiles + lists[e][0, b * degree + m]]
            first[e * tiles + b] = here + 0.15 * (total - 4.0 * here)
    for b in range(tiles):
        here = first[tiles + b]
        total = first[mine[0, b * degree]]
        for m in range(1, degree):
            total = total + first[mine[0, b * degree + m]]
        out[b] = here + 0.15 * (total - 4.0 * here)


def smooth(index, *parts):
    tiles, feat, cells = parts[0].shape
    return pl.pallas_call(
        smooth_kernel,
        out_shape=jax.ShapeDtypeStruct((tiles, feat, cells), jnp.float32),
        in_specs=[VMEM] * (1 + len(parts)),
        out_specs=VMEM,
        scratch_shapes=[
            pltpu.VMEM((5 * tiles, feat, cells), jnp.float32),
            pltpu.VMEM((3 * tiles, feat, cells), jnp.float32),
        ],
        compiler_params=PARAMS,
        cost_estimate=pl.CostEstimate(flops=2**20, bytes_accessed=2**20, transcendentals=0),
        name="smooth",
    )(index, *parts)


def shards(atm_blocks, send_list, weight_src, weights, ocean_nbrs):
    lists = send_list[0, 0]
    nbrs = ocean_nbrs[0, 0]
    groups, slots = lists.shape
    feat, cells = atm_blocks.shape[3:]
    tiles, degree = nbrs.shape
    count = lax.axis_size("dev")

    with jax.named_scope("pool"):
        picked, listed = pick(lists.T, nbrs, atm_blocks[0, 0])
        arrived = lax.all_to_all(picked, "grp", split_axis=0, concat_axis=0, tiled=True)
        arrived, listed = lax.optimization_barrier((arrived, listed))
        rows = groups * slots * feat
        own = jnp.concatenate([arrived.reshape(rows, cells), listed], axis=0)
        first = lax.ppermute(own, "dev", [(i, i ^ 1) for i in range(count)])
        second = lax.ppermute(own, "dev", [(i, ((i + 1) ^ 1) - 1) for i in range(1, count - 1)])
        listed = [part[rows : rows + 1, : tiles * degree] for part in (first, second, own)]
        state = remap(weight_src[0, 0], first, own, second, split(pltpu.with_memory_space_constraint(weights[0, 0], pltpu.HBM)), groups, slots, feat)

    with jax.named_scope("halo"):
        inner = lax.ppermute(state, "dev", [(i, i ^ 1) for i in range(count)])
        ring = lax.ppermute(state, "dev", [(i, i ^ 2) for i in range(count)])
        outer = lax.ppermute(state, "dev", [(i, ((i + 1) ^ 1) - 1) for i in range(1, count - 1)])
        across = lax.ppermute(state, "dev", [(i, ((i + 2) ^ 2) - 2) for i in range(2, count - 2)])

    with jax.named_scope("sweeps"):

        def listed_of(payload):
            return payload[rows : rows + 1, : tiles * degree].astype(jnp.int32)

        index = jnp.concatenate(listed, axis=0).astype(jnp.int32)
        state = smooth(index, state, inner, ring, across, outer)
    return state[None, None]


def solution(mesh):
    return jax.shard_map(
        shards,
        mesh=mesh,
        in_specs=(
            P("grp", "dev", None, None, None),
            P("grp", "dev", None, None),
            P("grp", "dev", None, None),
            P("grp", "dev", None, None, None, None),
            P("grp", "dev", None, None),
        ),
        out_specs=P("grp", "dev", None, None, None),
        check_vma=False,
    )
```

```python
import functools

import jax
import jax.numpy as jnp
from jax import lax
from jax.experimental import pallas as pl
from jax.experimental.pallas import tpu as pltpu
from jax.sharding import PartitionSpec as P

QUAD = 4
DEGREE = 4
VMEM = pl.BlockSpec(memory_space=pltpu.VMEM)
HBM = pl.BlockSpec(memory_space=pltpu.HBM)
PARAMS = pltpu.CompilerParams(vmem_limit_bytes=24 * 1024 * 1024)


def pick_kernel(lists, nbrs, atm, out, listed, chosen, beside, blocks, sems):
    first = pltpu.make_async_copy(lists, chosen, sems.at[0])
    second = pltpu.make_async_copy(nbrs, beside, sems.at[1])
    third = pltpu.make_async_copy(atm, blocks, sems.at[2])
    first.start()
    second.start()
    third.start()
    first.wait()
    second.wait()
    lane = lax.broadcasted_iota(jnp.int32, listed.shape, 1)
    row = jnp.zeros(listed.shape, jnp.int32)
    tiles, degree = beside.shape
    for b in range(tiles):
        for m in range(degree):
            row = jnp.where(lane == b * degree + m, beside[b, m], row)
    listed[...] = row.astype(jnp.float32)
    third.wait()
    for g in range(out.shape[0]):
        for c in range(out.shape[1]):
            out[g, c] = blocks[chosen[c, g]]


def pick(lists, nbrs, atm):
    slots, groups = lists.shape
    inputs = (pltpu.with_memory_space_constraint(a, pltpu.HBM) for a in (lists, nbrs, atm))
    return pl.pallas_call(
        pick_kernel,
        out_shape=[
            jax.ShapeDtypeStruct((groups, slots) + atm.shape[1:], jnp.float32),
            jax.ShapeDtypeStruct((8, atm.shape[2]), jnp.float32),
        ],
        in_specs=[HBM, HBM, HBM],
        out_specs=[VMEM, VMEM],
        scratch_shapes=[
            pltpu.SMEM(lists.shape, jnp.int32),
            pltpu.SMEM(nbrs.shape, jnp.int32),
            pltpu.VMEM(atm.shape, jnp.float32),
            pltpu.SemaphoreType.DMA((3,)),
        ],
        compiler_params=PARAMS,
        cost_estimate=pl.CostEstimate(flops=0, bytes_accessed=2**19, transcendentals=0),
        name="pick",
    )(*inputs)


def halves(x):
    high = x.astype(jnp.bfloat16)
    return high, (x - high.astype(jnp.float32)).astype(jnp.bfloat16)


def split_kernel(weights, out):
    tiles, blocks, depth, cells = weights.shape
    for b in range(tiles):
        out[b] = jnp.concatenate(halves(weights[b].reshape(blocks * depth, cells)), axis=1)


def split(weights):
    tiles, blocks, depth, cells = weights.shape
    return pl.pallas_call(
        split_kernel,
        out_shape=jax.ShapeDtypeStruct((tiles, blocks * depth, 2 * cells), jnp.bfloat16),
        in_specs=[VMEM],
        out_specs=VMEM,
        compiler_params=PARAMS,
        cost_estimate=pl.CostEstimate(flops=2**20, bytes_accessed=2**22, transcendentals=0),
        name="split",
    )(weights)


def remap_kernel(slots, source, first, own, second, weights, out, lists, pool):
    tiles, feat, cells = out.shape
    entries = pool.shape[0]
    chosen = source[...]
    swap = 2 * (1 - lax.rem(lax.axis_index("dev"), 2))
    for side, part in ((swap, first), (1, own), (2 - swap, second)):
        for entry in range(entries // 3):
            s, c = divmod(entry, slots)
            pool[(s * 3 + side) * slots + c] = part[entry * feat : (entry + 1) * feat, :]
    for row, part in enumerate((first, second, own)):
        lists[row] = part[entries // 3 * feat :, :].astype(jnp.int32)
    for b in range(tiles):
        left = jnp.concatenate([pool[chosen[b, k]] for k in range(source.shape[1])], axis=1)
        left = jnp.concatenate(halves(left), axis=0)
        product = jnp.dot(left, weights[b], preferred_element_type=jnp.float32)
        total = product[:feat, :cells] + (product[:feat, cells:] + product[feat:, :cells])
        out[b] = total


def remap(source, first, own, second, weights, groups, slots, feat):
    tiles, depth, width = weights.shape
    cells = width // 2
    return pl.pallas_call(
        functools.partial(remap_kernel, slots),
        out_shape=[
            jax.ShapeDtypeStruct((tiles, feat, cells), jnp.float32),
            jax.ShapeDtypeStruct((3, first.shape[0] - groups * slots * feat, cells), jnp.int32),
        ],
        in_specs=[VMEM] * 5,
        out_specs=[VMEM, VMEM],
        scratch_shapes=[pltpu.VMEM((3 * groups * slots, feat, cells), jnp.float32)],
        compiler_params=PARAMS,
        cost_estimate=pl.CostEstimate(flops=8 * tiles * feat * depth * cells, bytes_accessed=2**22, transcendentals=0),
        name="remap",
    )(source, first, own, second, weights)


def smooth_kernel(index, own, inner, ring, across, outer, out, state, first):
    tiles = out.shape[0]
    degree = DEGREE
    pair, other, mine = (index[row, :1, :] for row in range(3))
    place = lax.axis_index("dev")
    odd = lax.rem(place, 2) == 1
    upper = lax.rem(place, QUAD) >= 2
    after = jnp.where(odd, other, pair)
    after = jnp.where(place == lax.axis_size("dev") - 1, 3 * tiles - 1, after)
    lists = (jnp.where(odd, pair, other), mine, after)
    for t in range(tiles):
        state[t] = jnp.where(upper, ring[t], across[t])
        state[tiles + t] = jnp.where(odd, inner[t], outer[t])
        state[2 * tiles + t] = own[t]
        state[3 * tiles + t] = jnp.where(odd, outer[t], inner[t])
        state[4 * tiles + t] = jnp.where(upper, across[t], ring[t])
    for e in range(3):
        for b in range(tiles):
            here = state[(e + 1) * tiles + b]
            total = state[e * tiles + lists[e][0, b * degree]]
            for m in range(1, degree):
                total = total + state[e * tiles + lists[e][0, b * degree + m]]
            first[e * tiles + b] = here + 0.15 * (total - 4.0 * here)
    for b in range(tiles):
        here = first[tiles + b]
        total = first[mine[0, b * degree]]
        for m in range(1, degree):
            total = total + first[mine[0, b * degree + m]]
        out[b] = here + 0.15 * (total - 4.0 * here)


def smooth(index, *parts):
    tiles, feat, cells = parts[0].shape
    return pl.pallas_call(
        smooth_kernel,
        out_shape=jax.ShapeDtypeStruct((tiles, feat, cells), jnp.float32),
        in_specs=[VMEM] * (1 + len(parts)),
        out_specs=VMEM,
        scratch_shapes=[
            pltpu.VMEM((5 * tiles, feat, cells), jnp.float32),
            pltpu.VMEM((3 * tiles, feat, cells), jnp.float32),
        ],
        compiler_params=PARAMS,
        cost_estimate=pl.CostEstimate(flops=2**20, bytes_accessed=2**20, transcendentals=0),
        name="smooth",
    )(index, *parts)


def shards(atm_blocks, send_list, weight_src, weights, ocean_nbrs):
    lists = send_list[0, 0]
    nbrs = ocean_nbrs[0, 0]
    groups, slots = lists.shape
    feat, cells = atm_blocks.shape[3:]
    tiles, degree = nbrs.shape
    count = lax.axis_size("dev")

    with jax.named_scope("pool"):
        picked, listed = pick(lists.T, nbrs, atm_blocks[0, 0])
        arrived = lax.all_to_all(picked, "grp", split_axis=0, concat_axis=0, tiled=True)
        arrived, listed = lax.optimization_barrier((arrived, listed))
        rows = groups * slots * feat
        own = jnp.concatenate([arrived.reshape(rows, cells), listed], axis=0)
        first = lax.ppermute(own, "dev", [(i, i ^ 1) for i in range(count)])
        second = lax.ppermute(own, "dev", [(i, ((i + 1) ^ 1) - 1) for i in range(1, count - 1)])
        state, lists = remap(weight_src[0, 0], first, own, second, split(pltpu.with_memory_space_constraint(weights[0, 0], pltpu.HBM)), groups, slots, feat)

    with jax.named_scope("halo"):
        inner = lax.ppermute(state, "dev", [(i, i ^ 1) for i in range(count)])
        ring = lax.ppermute(state, "dev", [(i, i ^ 2) for i in range(count)])
        outer = lax.ppermute(state, "dev", [(i, ((i + 1) ^ 1) - 1) for i in range(1, count - 1)])
        across = lax.ppermute(state, "dev", [(i, ((i + 2) ^ 2) - 2) for i in range(2, count - 2)])

    with jax.named_scope("sweeps"):

        def listed_of(payload):
            return payload[rows : rows + 1, : tiles * degree].astype(jnp.int32)

        state = smooth(lists, state, inner, ring, across, outer)
    return state[None, None]


def solution(mesh):
    return jax.shard_map(
        shards,
        mesh=mesh,
        in_specs=(
            P("grp", "dev", None, None, None),
            P("grp", "dev", None, None),
            P("grp", "dev", None, None),
            P("grp", "dev", None, None, None, None),
            P("grp", "dev", None, None),
        ),
        out_specs=P("grp", "dev", None, None, None),
        check_vma=False,
    )
```

```python
import functools

import jax
import jax.numpy as jnp
from jax import lax
from jax.experimental import pallas as pl
from jax.experimental.pallas import tpu as pltpu
from jax.sharding import PartitionSpec as P

QUAD = 4
DEGREE = 4
VMEM = pl.BlockSpec(memory_space=pltpu.VMEM)
HBM = pl.BlockSpec(memory_space=pltpu.HBM)
PARAMS = pltpu.CompilerParams(vmem_limit_bytes=24 * 1024 * 1024)


def pick_kernel(lists, nbrs, atm, out, listed, chosen, beside, blocks, sems):
    first = pltpu.make_async_copy(lists, chosen, sems.at[0])
    second = pltpu.make_async_copy(nbrs, beside, sems.at[1])
    third = pltpu.make_async_copy(atm, blocks, sems.at[2])
    first.start()
    second.start()
    third.start()
    first.wait()
    second.wait()
    lane = lax.broadcasted_iota(jnp.int32, listed.shape, 1)
    row = jnp.zeros(listed.shape, jnp.int32)
    tiles, degree = beside.shape
    for b in range(tiles):
        for m in range(degree):
            row = jnp.where(lane == b * degree + m, beside[b, m], row)
    listed[...] = row.astype(jnp.float32)
    third.wait()
    for g in range(out.shape[0]):
        for c in range(out.shape[1]):
            out[g, c] = blocks[chosen[c, g]]


def pick(lists, nbrs, atm):
    slots, groups = lists.shape
    inputs = (pltpu.with_memory_space_constraint(a, pltpu.HBM) for a in (lists, nbrs, atm))
    return pl.pallas_call(
        pick_kernel,
        out_shape=[
            jax.ShapeDtypeStruct((groups, slots) + atm.shape[1:], jnp.float32),
            jax.ShapeDtypeStruct((8, atm.shape[2]), jnp.float32),
        ],
        in_specs=[HBM, HBM, HBM],
        out_specs=[VMEM, VMEM],
        scratch_shapes=[
            pltpu.SMEM(lists.shape, jnp.int32),
            pltpu.SMEM(nbrs.shape, jnp.int32),
            pltpu.VMEM(atm.shape, jnp.float32),
            pltpu.SemaphoreType.DMA((3,)),
        ],
        compiler_params=PARAMS,
        cost_estimate=pl.CostEstimate(flops=0, bytes_accessed=2**19, transcendentals=0),
        name="pick",
    )(*inputs)


def halves(x):
    high = x.astype(jnp.bfloat16)
    return high, (x - high.astype(jnp.float32)).astype(jnp.bfloat16)


def split_kernel(weights, out):
    tiles, blocks, depth, cells = weights.shape
    for b in range(tiles):
        out[b] = jnp.concatenate(halves(weights[b].reshape(blocks * depth, cells)), axis=1)


def split(weights):
    tiles, blocks, depth, cells = weights.shape
    return pl.pallas_call(
        split_kernel,
        out_shape=jax.ShapeDtypeStruct((tiles, blocks * depth, 2 * cells), jnp.bfloat16),
        in_specs=[VMEM],
        out_specs=VMEM,
        compiler_params=PARAMS,
        cost_estimate=pl.CostEstimate(flops=2**20, bytes_accessed=2**22, transcendentals=0),
        name="split",
    )(weights)


def remap_kernel(slots, source, first, own, second, weights, out, lists, pool):
    tiles, feat, cells = out.shape
    entries = pool.shape[0]
    chosen = source[...]
    swap = 2 * (1 - lax.rem(lax.axis_index("dev"), 2))
    for side, part in ((swap, first), (1, own), (2 - swap, second)):
        for entry in range(entries // 3):
            s, c = divmod(entry, slots)
            pool[(s * 3 + side) * slots + c] = part[entry * feat : (entry + 1) * feat, :]
    for row, part in enumerate((first, second, own)):
        lists[row] = part[entries // 3 * feat :, :].astype(jnp.int32)
    for b in range(tiles):
        left = jnp.concatenate([pool[chosen[b, k]] for k in range(source.shape[1])], axis=1)
        left = jnp.concatenate(halves(left), axis=0)
        product = jnp.dot(left, weights[b], preferred_element_type=jnp.float32)
        total = product[:feat, :cells] + (product[:feat, cells:] + product[feat:, :cells])
        out[b] = total


def remap(source, first, own, second, weights, groups, slots, feat):
    tiles, depth, width = weights.shape
    cells = width // 2
    return pl.pallas_call(
        functools.partial(remap_kernel, slots),
        out_shape=[
            jax.ShapeDtypeStruct((tiles, feat, cells), jnp.float32),
            jax.ShapeDtypeStruct((3, first.shape[0] - groups * slots * feat, cells), jnp.int32),
        ],
        in_specs=[VMEM] * 5,
        out_specs=[VMEM, VMEM],
        scratch_shapes=[pltpu.VMEM((3 * groups * slots, feat, cells), jnp.float32)],
        compiler_params=PARAMS,
        cost_estimate=pl.CostEstimate(flops=8 * tiles * feat * depth * cells, bytes_accessed=2**22, transcendentals=0),
        name="remap",
    )(source, first, own, second, weights)


def smooth_kernel(index, own, inner, ring, outer, across, out, state, first):
    tiles = out.shape[0]
    degree = DEGREE
    pair, other, mine = (index[row, :1, :] for row in range(3))
    place = lax.axis_index("dev")
    odd = lax.rem(place, 2) == 1
    upper = lax.rem(place, QUAD) >= 2
    after = jnp.where(odd, other, pair)
    after = jnp.where(place == lax.axis_size("dev") - 1, 3 * tiles - 1, after)
    lists = (jnp.where(odd, pair, other), mine, after)
    for t in range(tiles):
        state[t] = jnp.where(upper, ring[t], across[t])
        state[tiles + t] = jnp.where(odd, inner[t], outer[t])
        state[2 * tiles + t] = own[t]
        state[3 * tiles + t] = jnp.where(odd, outer[t], inner[t])
        state[4 * tiles + t] = jnp.where(upper, across[t], ring[t])
    for e in range(3):
        for b in range(tiles):
            here = state[(e + 1) * tiles + b]
            total = state[e * tiles + lists[e][0, b * degree]]
            for m in range(1, degree):
                total = total + state[e * tiles + lists[e][0, b * degree + m]]
            first[e * tiles + b] = here + 0.15 * (total - 4.0 * here)
    for b in range(tiles):
        here = first[tiles + b]
        total = first[mine[0, b * degree]]
        for m in range(1, degree):
            total = total + first[mine[0, b * degree + m]]
        out[b] = here + 0.15 * (total - 4.0 * here)


def smooth(index, *parts):
    tiles, feat, cells = parts[0].shape
    return pl.pallas_call(
        smooth_kernel,
        out_shape=jax.ShapeDtypeStruct((tiles, feat, cells), jnp.float32),
        in_specs=[VMEM] * (1 + len(parts)),
        out_specs=VMEM,
        scratch_shapes=[
            pltpu.VMEM((5 * tiles, feat, cells), jnp.float32),
            pltpu.VMEM((3 * tiles, feat, cells), jnp.float32),
        ],
        compiler_params=PARAMS,
        cost_estimate=pl.CostEstimate(flops=2**20, bytes_accessed=2**20, transcendentals=0),
        name="smooth",
    )(index, *parts)


def shards(atm_blocks, send_list, weight_src, weights, ocean_nbrs):
    lists = send_list[0, 0]
    nbrs = ocean_nbrs[0, 0]
    groups, slots = lists.shape
    feat, cells = atm_blocks.shape[3:]
    tiles, degree = nbrs.shape
    count = lax.axis_size("dev")

    with jax.named_scope("pool"):
        picked, listed = pick(lists.T, nbrs, atm_blocks[0, 0])
        arrived = lax.all_to_all(picked, "grp", split_axis=0, concat_axis=0, tiled=True)
        arrived, listed = lax.optimization_barrier((arrived, listed))
        rows = groups * slots * feat
        own = jnp.concatenate([arrived.reshape(rows, cells), listed], axis=0)
        first = lax.ppermute(own, "dev", [(i, i ^ 1) for i in range(count)])
        second = lax.ppermute(own, "dev", [(i, ((i + 1) ^ 1) - 1) for i in range(1, count - 1)])
        state, lists = remap(weight_src[0, 0], first, own, second, split(pltpu.with_memory_space_constraint(weights[0, 0], pltpu.HBM)), groups, slots, feat)

    with jax.named_scope("halo"):
        inner = lax.ppermute(state, "dev", [(i, i ^ 1) for i in range(count)])
        ring = lax.ppermute(state, "dev", [(i, i ^ 2) for i in range(count)])
        outer = lax.ppermute(state, "dev", [(i, ((i + 1) ^ 1) - 1) for i in range(1, count - 1)])
        across = lax.ppermute(state, "dev", [(i, ((i + 2) ^ 2) - 2) for i in range(2, count - 2)])

    with jax.named_scope("sweeps"):

        def listed_of(payload):
            return payload[rows : rows + 1, : tiles * degree].astype(jnp.int32)

        state = smooth(lists, state, inner, ring, outer, across)
    return state[None, None]


def solution(mesh):
    return jax.shard_map(
        shards,
        mesh=mesh,
        in_specs=(
            P("grp", "dev", None, None, None),
            P("grp", "dev", None, None),
            P("grp", "dev", None, None),
            P("grp", "dev", None, None, None, None),
            P("grp", "dev", None, None),
        ),
        out_specs=P("grp", "dev", None, None, None),
        check_vma=False,
    )
```
